32 devices in a mesh: lon: 4 (over y, x), lat: 8 (over z, core).
Axes of the slice: x: 2, y: 2, z: 4, core: 2. Of those that a mesh axis runs over, the one named last changes fastest.
Arguments:
- fields: float32 [8, 8, 240, 2880], P(None, None, 'lat', 'lon'), may hold values from -6 to 6
- mask: int32 [240], P('lat'), may hold values from 0 to 1, as said below
- cutoff: int32 [240], P('lat'), may hold values from 1 to 128, as said below
Outputs:
- updated: float32 [8, 8, 240, 2880], P(None, None, 'lat', 'lon')
The draws below stay inside these ranges and needn't reach their ends.
Inputs may be any that keep to these rules, and one draw needn't show every extreme that they name: `mask`: nonzero only within 40 rows of either pole; row 0 is always 1. `cutoff`: both ends are taken in every draw.
All inputs are finite; a program needn't handle non-finite values.
Results may differ from the reference program's by a relative error of at most 0.00005.
Values sent between devices are 32-bit elements; how exact they have to be, the bound alone decides.
A program may use at most 64 MiB of HBM per device.

```python
import math
import jax
import jax.numpy as jnp
from jax import lax

NFIELDS = 8
NLON = 2880
KMAX = 128
LEV = 8
NLAT = 240
CAP = 40


def draw_mask(key, part):
    rows = jnp.arange(NLAT)
    coin = jax.random.randint(key, (NLAT,), 0, 4)
    polar = (rows < CAP) | (rows >= NLAT - CAP)
    chosen = jnp.where(polar & (coin != 0), 1, 0)
    return jnp.where(rows == 0, 1, chosen).astype(jnp.int32)


def draw_cutoff(key, part):
    rows = jnp.arange(NLAT)
    values = jax.random.randint(key, (NLAT,), 1, KMAX + 1)
    picked = jax.random.randint(jax.random.fold_in(key, 7), (), 0, NLAT)
    values = jnp.where(rows == picked, KMAX, values)
    values = jnp.where(rows == (picked + 1) % NLAT, 1, values)
    return values.astype(jnp.int32)


def shard_levels(rng, extent, cuts, least, top_value):
    factor_of, own = 1.0, jax.random.fold_in(rng, 6)
    for axis_at, shards_of in cuts:
        heights = jnp.exp(jax.random.uniform(jax.random.fold_in(own, axis_at), (shards_of,), jnp.float32, least / len(cuts), top_value / len(cuts)))
        factor_of = factor_of * jnp.repeat(heights, extent[axis_at] // shards_of).reshape([-1 if axis == axis_at else 1 for axis in range(len(extent))])
    return factor_of


def noise(stream_key, shape, spread, bound, pieces=(), held_as=jnp.bfloat16):
    array = spread * jax.random.normal(stream_key, shape, jnp.float32)
    if pieces:
        array = array * shard_levels(stream_key, shape, pieces, -0.22, 0.18)
    return jnp.clip(array, -bound, bound).astype(held_as)


def setup_inputs(seed: int = 0) -> dict:
    keys = jax.random.split(jax.random.key(seed), 4)
    return {
        "fields": noise(keys[0], (NFIELDS, LEV, NLAT, NLON), 1.0, 6.0, ((2, 8), (3, 4)), jnp.float32),
        "mask": draw_mask(jax.random.fold_in(keys[3], 71), 0),
        "cutoff": draw_cutoff(jax.random.fold_in(keys[3], 71), 0),
    }


def tendencies(north, south, east, west, cos_north, cos_south, dlon, dlat):
    press_t = -((east[1] - west[1]) / (2.0 * dlon) + (cos_north * north[2] - cos_south * south[2]) / (2.0 * dlat))
    zonal_t = -(east[0] - west[0]) / (2.0 * dlon)
    merid_t = -(north[0] - south[0]) / (2.0 * dlat)
    scalar_t = -((east[1] * east[3:] - west[1] * west[3:]) / (2.0 * dlon)
                 + (cos_north * north[2] * north[3:] - cos_south * south[2] * south[3:]) / (2.0 * dlat))
    return jnp.concatenate([press_t[None], zonal_t[None], merid_t[None], scalar_t], axis=0)


def reference(fields, mask, cutoff):
    dlon = 2.0 * math.pi / NLON
    dlat = math.pi / NLAT
    step = 0.4 * dlon
    index = jnp.arange(NFIELDS)
    signs = jnp.where((index == 1) | (index == 2), -1.0, 1.0).astype(jnp.float32)[:, None]
    rows = jnp.clip(jnp.arange(NLAT + 2) - 1, 0, NLAT - 1)
    cosine = jnp.cos(-math.pi / 2 + (rows.astype(jnp.float32) + 0.5) * dlat).astype(jnp.float32)
    cos_north = cosine[2:][:, None]
    cos_south = cosine[:-2][:, None]
    wavenum = jnp.arange(NLON // 2 + 1)
    keep = (wavenum[None, :] < cutoff[:, None]).astype(jnp.float32)
    maskf = mask.astype(jnp.float32)[:, None]

    def one_level(level):
        low = jnp.roll(level[:, 0, :], NLON // 2, axis=-1) * signs
        high = jnp.roll(level[:, -1, :], NLON // 2, axis=-1) * signs
        padded = jnp.concatenate([low[:, None], level, high[:, None]], axis=1)
        east = jnp.roll(level, -1, axis=2)
        west = jnp.roll(level, 1, axis=2)
        tend = tendencies(padded[:, 2:], padded[:, :-2], east, west, cos_north, cos_south, dlon, dlat)
        spec = jnp.fft.rfft(tend, axis=-1)
        proj = jnp.fft.irfft(spec * keep[None], n=NLON, axis=-1).astype(tend.dtype)
        filtered = tend + maskf[None] * (proj - tend)
        return level + step * filtered

    out = lax.map(one_level, jnp.transpose(fields, (1, 0, 2, 3)))
    return jnp.transpose(out, (1, 0, 2, 3))
```

```python
import functools
import math

import jax
import jax.numpy as jnp
import ml_dtypes
import numpy as np
from jax import lax
from jax.experimental import pallas as pl
from jax.experimental.pallas import tpu as pltpu
from jax.sharding import PartitionSpec as P

KMAX = 128
F32, BF16 = jnp.float32, jnp.bfloat16
NT = (((1,), (1,)), ((), ()))
NN = (((1,), (0,)), ((), ()))
TN = (((0,), (0,)), ((), ()))


def split_np(a):
    hi = a.astype(ml_dtypes.bfloat16)
    lo = (a - hi.astype(np.float64)).astype(ml_dtypes.bfloat16)
    return hi, lo


def split(a):
    hi = a.astype(BF16)
    return hi, (a - hi.astype(F32)).astype(BF16)


def dot(a, b, dims):
    return lax.dot_general(a, b, dims, preferred_element_type=F32)


@functools.lru_cache(maxsize=None)
def factors(nlon, width):
    source, target, ranks = [], [], []
    for off in range(1, nlon // width):
        gaps = np.array(
            [1.0 / (nlon * math.sin((off * width + d) * math.pi / nlon)) for d in range(1 - width, width)]
        )
        idx = np.arange(width)
        rest = gaps[idx[:, None] - idx[None, :] + width - 1]
        bias = 1.0 + 1e-6 * idx[:, None] / width
        src, tgt = [], []
        while len(src) % 8 or not src or np.abs(rest).max() > 1e-9:
            i, j = np.unravel_index(np.argmax(np.abs(rest) * bias), rest.shape)
            row, col = rest[i] / rest[i, j], rest[:, j].copy()
            src.append(row)
            tgt.append(col)
            rest = rest - col[:, None] * row[None, :]
        ranks.append(len(src))
        source += src
        target += tgt
    return np.stack(source), np.stack(target), tuple(ranks)


def first_kernel(ranks, a, b, f_ref, side_ref, low_ref, high_ref, cos_ref, c_ref, s_ref, u_ref, t_ref, *rest):
    h_refs, w = rest[:-1], rest[-1]
    nf, rows, lon = f_ref.shape[0], f_ref.shape[2], f_ref.shape[3]
    frame, wide = w.shape[1], w.shape[2]
    for f in range(nf):
        w[f, 1 : rows + 1, 0:lon] = f_ref[f, 0]
        w[f, 0:1, 0:lon] = low_ref[0, f : f + 1]
        w[f, rows + 1 : rows + 2, 0:lon] = high_ref[0, f : f + 1]
        w[f, :, lon:wide] = side_ref[0, f]

    def dx(z):
        return pltpu.roll(z, wide - 1, 1) - pltpu.roll(z, 1, 1)

    def dy(z):
        return pltpu.roll(z, frame - 1, 0) - pltpu.roll(z, 1, 0)

    ua = w[1] * (-a)
    cv = w[2] * (cos_ref[:, 0:1] * (-b))
    tend = [dx(ua) + dy(cv), dx(w[0]) * (-a), dy(w[0]) * (-b)]
    for f in range(3, nf):
        tend.append(dx(ua * w[f]) + dy(cv * w[f]))
    parts = []
    for table in (c_ref[...], s_ref[...]):
        pairs = [split(t * table) for t in tend]
        hi = jnp.concatenate([p[0] for p in pairs], axis=0)
        lo = jnp.concatenate([p[1] for p in pairs], axis=0)
        n = u_ref.shape[0] // 2
        both = dot(u_ref[...], hi, NT)
        parts.append(both[:n] + both[n:] + dot(u_ref[0:n], lo, NT))
    for f in range(nf):
        t_ref[f, 0] = tend[f][:, 0:lon]
    at = 0
    for h_ref, r in zip(h_refs, ranks):
        h_ref[0, 0:r] = parts[0][at : at + r]
        h_ref[0, r : 2 * r] = parts[1][at : at + r]
        at += r


def second_kernel(ranks, f_ref, t_ref, c_ref, s_ref, keep_ref, wt_ref, thi, tlo, ihi, ilo, v_ref, *rest):
    h_refs, o_ref = rest[:-1], rest[-1]
    nf, rows, lon = f_ref.shape[0], f_ref.shape[2], f_ref.shape[3]
    frame = t_ref.shape[2]
    tend = jnp.concatenate([t_ref[f, 0] for f in range(nf)], axis=0)
    hi, lo = split(tend)
    spec = dot(hi, thi[...], NN) + dot(hi, tlo[...], NN) + dot(lo, thi[...], NN)
    spec = jnp.concatenate(
        [spec[f * frame : (f + 1) * frame] * wt_ref[...] for f in range(nf)], axis=0
    )
    hi, lo = split(spec)
    local = dot(hi, ihi[...], NN) + dot(hi, ilo[...], NN) + dot(lo, ihi[...], NN)
    far = []
    for part in range(2):
        h = jnp.concatenate([ref[0, part * r : (part + 1) * r] for ref, r in zip(h_refs, ranks)], axis=0)
        h = jnp.concatenate([h, jnp.zeros((v_ref.shape[0] // 3 - h.shape[0], h.shape[1]), F32)], axis=0) if v_ref.shape[0] // 3 > h.shape[0] else h
        hi, lo = split(h)
        far.append(dot(jnp.concatenate([hi, lo, hi], axis=0), v_ref[...], TN))
    for f in range(nf):
        at = slice(f * frame, (f + 1) * frame)
        add = local[at] + far[0][at] * s_ref[...] - far[1][at] * c_ref[...] + t_ref[f, 0] * keep_ref[:, 0:1]
        o_ref[f, 0] = f_ref[f, 0] + add[1 : rows + 1]


def shards(fields, mask, cutoff):
    nf, nlev, rows, lon = fields.shape
    lon_count = lax.axis_size("lon")
    lat_count = lax.axis_size("lat")
    nlon, nlat = lon * lon_count, rows * lat_count
    dlon, dlat = 2.0 * math.pi / nlon, math.pi / nlat
    step = 0.4 * dlon
    lat_pos, lon_pos = lax.axis_index("lat"), lax.axis_index("lon")
    frame = -(-(rows + 2) // 8) * 8
    wide = -(-(lon + 2) // 128) * 128
    source, target, ranks = factors(nlon, lon)
    total = sum(ranks)
    padr = -(-total // 16) * 16

    index = jnp.arange(nf)
    signs = jnp.where((index == 1) | (index == 2), -1.0, 1.0).astype(F32)[None, :, None]
    first = jnp.transpose(fields[:, :, 0, :], (1, 0, 2))
    last = jnp.transpose(fields[:, :, -1, :], (1, 0, 2))
    up = [(i, i + 1) for i in range(lat_count - 1)]
    down = [(j, i) for i, j in up]

    def around(x, off):
        return lax.ppermute(x, "lon", [(i, (i + off) % lon_count) for i in range(lon_count)])

    across = around(jnp.where(lat_pos == 0, first, last), lon_count // 2) * signs
    low = jnp.where(lat_pos == 0, across, lax.ppermute(last, "lat", up))
    high = jnp.where(lat_pos == lat_count - 1, across, lax.ppermute(first, "lat", down))
    edge_w = jnp.transpose(fields[:, :, :, 0], (1, 0, 2))
    edge_e = jnp.transpose(fields[:, :, :, -1], (1, 0, 2))
    east = around(edge_w, -1)
    west = around(edge_e, 1)
    side_w = wide - lon
    lane = jnp.arange(side_w)
    pad = ((0, 0), (0, 0), (1, frame - rows - 1))
    east, west = jnp.pad(east, pad)[..., None], jnp.pad(west, pad)[..., None]
    side = jnp.where(lane == 0, east, jnp.where(lane == side_w - 1, west, 0.0))

    rowid = jnp.clip(lat_pos * rows + jnp.arange(frame) - 1, 0, nlat - 1)
    cosine = jnp.cos(-math.pi / 2 + (rowid.astype(F32) + 0.5) * dlat)
    cosine = jnp.broadcast_to(cosine[:, None], (frame, 128))
    vpad = (1, frame - rows - 1)
    cut = jnp.pad(cutoff, vpad, constant_values=1)
    on = jnp.pad(mask.astype(F32), vpad) * step
    cols = lon_pos * lon + jnp.arange(wide, dtype=jnp.int32)
    turn = ((2 * cut[:, None] - 1) * cols[None, :]) % (2 * nlon)
    phase = turn.astype(F32) * (math.pi / nlon)
    inside = (jnp.arange(wide) < lon).astype(F32)
    cphase, sphase = jnp.cos(phase) * inside, jnp.sin(phase) * inside
    con, son = cphase[:, :lon] * on[:, None], sphase[:, :lon] * on[:, None]
    keep = jnp.broadcast_to((step - on)[:, None], (frame, 128))
    wavenum = jnp.arange(KMAX)
    scale = jnp.where(wavenum == 0, 1.0 / nlon, 2.0 / nlon).astype(F32)
    weights = (wavenum[None, :] < cut[:, None]).astype(F32) * scale[None, :] * on[:, None]
    weights = jnp.concatenate([weights, weights], axis=1)

    u = np.zeros((padr, wide))
    u[:total, :lon] = source
    u = np.concatenate(split_np(u), axis=0)
    v = np.zeros((padr, lon))
    v[:total] = target
    vhi, vlo = split_np(v)
    flip, at = [], 0
    for off, r in zip(range(1, lon_count), ranks):
        flip.append(jnp.where(lon_pos >= off, 1.0, -1.0) * jnp.ones((r,)))
    flip = jnp.concatenate(flip + [jnp.ones((padr - total,))])
    flip = jnp.concatenate([flip] * 3).astype(BF16)[:, None]
    v = jnp.asarray(np.concatenate([vhi, vhi, vlo], axis=0)) * flip
    angle = (np.arange(lon)[:, None] * np.arange(KMAX)[None, :] % nlon) * (2.0 * math.pi / nlon)
    table = np.concatenate([np.cos(angle), np.sin(angle)], axis=1)
    thi, tlo = split_np(table)
    ihi, ilo = np.ascontiguousarray(thi.T), np.ascontiguousarray(tlo.T)

    def whole(x):
        return pl.BlockSpec(x.shape, lambda l: (0,) * x.ndim)

    def level(*shape):
        return pl.BlockSpec((1,) + shape, lambda l: (l,) + (0,) * len(shape))

    def by_level(r, c):
        return pl.BlockSpec((nf, 1, r, c), lambda l: (0, l, 0, 0))

    m = nf * frame
    params = pltpu.CompilerParams(vmem_limit_bytes=32 * 1024 * 1024)
    shared = [cosine, cphase, sphase, jnp.asarray(u)]
    out = pl.pallas_call(
        functools.partial(first_kernel, ranks, 1.0 / (2.0 * dlon), 1.0 / (2.0 * dlat)),
        grid=(nlev,),
        in_specs=[by_level(rows, lon), level(nf, frame, side_w), level(nf, lon), level(nf, lon)]
        + [whole(x) for x in shared],
        out_specs=[by_level(frame, lon)] + [level(2 * r, m) for r in ranks],
        out_shape=[jax.ShapeDtypeStruct((nf, nlev, frame, lon), F32)]
        + [jax.ShapeDtypeStruct((nlev, 2 * r, m), F32) for r in ranks],
        scratch_shapes=[pltpu.VMEM((nf, frame, wide), F32)],
        compiler_params=params,
        name="tendency",
    )(fields, side, low, high, *shared)
    tend, sent = out[0], out[1:]
    got = [around(h, off) for off, h in zip(range(1, lon_count), sent)]
    shared = [con, son, keep, weights, jnp.asarray(thi), jnp.asarray(tlo), jnp.asarray(ihi), jnp.asarray(ilo), v]
    return pl.pallas_call(
        functools.partial(second_kernel, ranks),
        grid=(nlev,),
        in_specs=[by_level(rows, lon), by_level(frame, lon)]
        + [whole(x) for x in shared]
        + [level(2 * r, m) for r in ranks],
        out_specs=by_level(rows, lon),
        out_shape=jax.ShapeDtypeStruct(fields.shape, F32),
        compiler_params=params,
        name="projection",
    )(fields, tend, *shared, *got)


def solution(mesh):
    placed = (P(None, None, "lat", "lon"), P("lat"), P("lat"))
    return jax.shard_map(
        shards, mesh=mesh, in_specs=placed, out_specs=P(None, None, "lat", "lon"), check_vma=False
    )
```

```python
import functools
import math

import jax
import jax.numpy as jnp
import ml_dtypes
import numpy as np
from jax import lax
from jax.experimental import pallas as pl
from jax.experimental.pallas import tpu as pltpu
from jax.sharding import PartitionSpec as P

KMAX = 128
F32, BF16 = jnp.float32, jnp.bfloat16
NT = (((1,), (1,)), ((), ()))
NN = (((1,), (0,)), ((), ()))
TN = (((0,), (0,)), ((), ()))


def split_np(a):
    hi = a.astype(ml_dtypes.bfloat16)
    lo = (a - hi.astype(np.float64)).astype(ml_dtypes.bfloat16)
    return hi, lo


def split(a):
    hi = a.astype(BF16)
    return hi, (a - hi.astype(F32)).astype(BF16)


def dot(a, b, dims):
    return lax.dot_general(a, b, dims, preferred_element_type=F32)


@functools.lru_cache(maxsize=None)
def factors(nlon, width):
    source, target, ranks = [], [], []
    for off in range(1, nlon // width):
        gaps = np.array(
            [1.0 / (nlon * math.sin((off * width + d) * math.pi / nlon)) for d in range(1 - width, width)]
        )
        idx = np.arange(width)
        rest = gaps[idx[:, None] - idx[None, :] + width - 1]
        bias = 1.0 + 1e-6 * idx[:, None] / width
        src, tgt = [], []
        while len(src) % 8 or not src or np.abs(rest).max() > 1e-9:
            i, j = np.unravel_index(np.argmax(np.abs(rest) * bias), rest.shape)
            row, col = rest[i] / rest[i, j], rest[:, j].copy()
            src.append(row)
            tgt.append(col)
            rest = rest - col[:, None] * row[None, :]
        ranks.append(len(src))
        source += src
        target += tgt
    return np.stack(source), np.stack(target), tuple(ranks)


def per_level(table, nlev):
    return jnp.concatenate(
        [jnp.broadcast_to(table[r : r + 1], (nlev, table.shape[1])) for r in range(table.shape[0])], axis=0
    )


def first_kernel(
    ranks, a, b, f_ref, prev_ref, next_ref, low_ref, high_ref, east_ref, west_ref,
    cos_ref, c_ref, s_ref, u_ref, t_ref, *rest
):
    h_refs, w = rest[:-1], rest[-1]
    nf, chunk, nlev, lon = f_ref.shape
    wide = w.shape[3]
    here, steps = pl.program_id(0), pl.num_programs(0)
    flat = (chunk * nlev, wide)

    @pl.when(here == 0)
    def _():
        w[:, :, :, lon:wide] = jnp.zeros((nf, chunk + 2, nlev, wide - lon), F32)

    for f in range(nf):
        w[f, 1 : chunk + 1, :, 0:lon] = f_ref[f]
        w[f, 0, :, 0:lon] = jnp.where(here == 0, low_ref[f], prev_ref[f, 0])
        w[f, chunk + 1, :, 0:lon] = jnp.where(here == steps - 1, high_ref[f], next_ref[f, 0])
        for r in range(chunk):
            k = f * chunk + r
            w[f, r + 1, :, lon : lon + 1] = east_ref[0, :, k : k + 1]
            w[f, r + 1, :, wide - 1 : wide] = west_ref[0, :, k : k + 1]

    def mid(f):
        return w[f, 1 : chunk + 1].reshape(flat)

    def dx(z):
        return pltpu.roll(z, wide - 1, 1) - pltpu.roll(z, 1, 1)

    def dy(z):
        return (z[2:] - z[:-2]).reshape(flat)

    ua = mid(1) * (-a)
    cv = w[2] * (cos_ref[0][:, :, 0:1] * (-b))
    tend = [dx(ua) + dy(cv), dx(mid(0)) * (-a), dy(w[0]) * (-b)]
    for f in range(3, nf):
        tend.append(dx(ua * mid(f)) + dy(cv * w[f]))
    parts = []
    for table in (per_level(c_ref[0], nlev), per_level(s_ref[0], nlev)):
        pairs = [split(t * table) for t in tend]
        hi = jnp.concatenate([p[0] for p in pairs], axis=0)
        lo = jnp.concatenate([p[1] for p in pairs], axis=0)
        n = u_ref.shape[0] // 2
        both = dot(u_ref[...], hi, NT)
        parts.append(both[:n] + both[n:] + dot(u_ref[0:n], lo, NT))
    for f in range(nf):
        t_ref[f] = tend[f][:, 0:lon].reshape(chunk, nlev, lon)
    at = 0
    for h_ref, r in zip(h_refs, ranks):
        h_ref[0, 0:r] = parts[0][at : at + r]
        h_ref[0, r : 2 * r] = parts[1][at : at + r]
        at += r


def second_kernel(ranks, f_ref, t_ref, c_ref, s_ref, keep_ref, wt_ref, thi, tlo, ihi, ilo, v_ref, *rest):
    h_refs, o_ref = rest[:-1], rest[-1]
    nf, chunk, nlev, lon = f_ref.shape
    m = chunk * nlev
    tend = [t_ref[f].reshape(m, lon) for f in range(nf)]
    hi, lo = split(jnp.concatenate(tend, axis=0))
    spec = dot(hi, thi[...], NN) + dot(hi, tlo[...], NN) + dot(lo, thi[...], NN)
    wt = per_level(wt_ref[0], nlev)
    spec = jnp.concatenate([spec[f * m : (f + 1) * m] * wt for f in range(nf)], axis=0)
    hi, lo = split(spec)
    local = dot(hi, ihi[...], NN) + dot(hi, ilo[...], NN) + dot(lo, ihi[...], NN)
    far = []
    spare = v_ref.shape[0] // 3 - sum(ranks)
    for part in range(2):
        h = [ref[0, part * r : (part + 1) * r] for ref, r in zip(h_refs, ranks)]
        if spare:
            h.append(jnp.zeros((spare, nf * m), F32))
        hi, lo = split(jnp.concatenate(h, axis=0))
        far.append(dot(jnp.concatenate([hi, lo, hi], axis=0), v_ref[...], TN))
    c, s, keep = (per_level(x[0], nlev) for x in (c_ref, s_ref, keep_ref))
    for f in range(nf):
        at = slice(f * m, (f + 1) * m)
        add = local[at] + far[0][at] * s - far[1][at] * c + tend[f] * keep
        o_ref[f] = f_ref[f] + add.reshape(chunk, nlev, lon)


def shards(fields, mask, cutoff):
    fields = jnp.transpose(fields, (0, 2, 1, 3))
    nf, rows, nlev, lon = fields.shape
    chunk = max(c for c in range(1, 7) if rows % c == 0)
    steps = rows // chunk
    lon_count = lax.axis_size("lon")
    lat_count = lax.axis_size("lat")
    nlon, nlat = lon * lon_count, rows * lat_count
    dlon, dlat = 2.0 * math.pi / nlon, math.pi / nlat
    step = 0.4 * dlon
    lat_pos, lon_pos = lax.axis_index("lat"), lax.axis_index("lon")
    wide = -(-(lon + 2) // 128) * 128
    source, target, ranks = factors(nlon, lon)
    total = sum(ranks)
    padr = -(-total // 16) * 16

    index = jnp.arange(nf)
    signs = jnp.where((index == 1) | (index == 2), -1.0, 1.0).astype(F32)[:, None, None]
    first = fields[:, 0]
    last = fields[:, -1]
    up = [(i, i + 1) for i in range(lat_count - 1)]
    down = [(j, i) for i, j in up]

    def around(x, off):
        return lax.ppermute(x, "lon", [(i, (i + off) % lon_count) for i in range(lon_count)])

    across = around(jnp.where(lat_pos == 0, first, last), lon_count // 2) * signs
    low = jnp.where(lat_pos == 0, across, lax.ppermute(last, "lat", up))
    high = jnp.where(lat_pos == lat_count - 1, across, lax.ppermute(first, "lat", down))

    def columns(x):
        return x.reshape(nf, steps, chunk, nlev).transpose(1, 3, 0, 2).reshape(steps, nlev, nf * chunk)

    east = around(columns(fields[:, :, :, 0]), -1)
    west = around(columns(fields[:, :, :, -1]), 1)

    rowid = np.arange(steps)[:, None] * chunk + np.arange(chunk + 2)[None, :] - 1
    rowid = jnp.clip(lat_pos * rows + rowid, 0, nlat - 1)
    cosine = jnp.cos(-math.pi / 2 + (rowid.astype(F32) + 0.5) * dlat)
    cosine = jnp.broadcast_to(cosine[:, :, None, None], (steps, chunk + 2, nlev, 128))
    cut = cutoff.reshape(steps, chunk)
    on = mask.astype(F32).reshape(steps, chunk) * step
    cols = lon_pos * lon + jnp.arange(wide, dtype=jnp.int32)
    turn = ((2 * cut[:, :, None] - 1) * cols) % (2 * nlon)
    phase = turn.astype(F32) * (math.pi / nlon)
    inside = (jnp.arange(wide) < lon).astype(F32)
    cphase, sphase = jnp.cos(phase) * inside, jnp.sin(phase) * inside
    con, son = cphase[:, :, :lon] * on[:, :, None], sphase[:, :, :lon] * on[:, :, None]
    keep = jnp.broadcast_to((step - on)[:, :, None], (steps, chunk, lon))
    wavenum = jnp.arange(KMAX)
    scale = jnp.where(wavenum == 0, 1.0 / nlon, 2.0 / nlon).astype(F32)
    weights = (wavenum < cut[:, :, None]).astype(F32) * scale * on[:, :, None]
    weights = jnp.concatenate([weights, weights], axis=2)

    u = np.zeros((padr, wide))
    u[:total, :lon] = source
    u = np.concatenate(split_np(u), axis=0)
    v = np.zeros((padr, lon))
    v[:total] = target
    vhi, vlo = split_np(v)
    flip, at = [], 0
    for off, r in zip(range(1, lon_count), ranks):
        flip.append(jnp.where(lon_pos >= off, 1.0, -1.0) * jnp.ones((r,)))
    flip = jnp.concatenate(flip + [jnp.ones((padr - total,))])
    flip = jnp.concatenate([flip] * 3).astype(BF16)[:, None]
    v = jnp.asarray(np.concatenate([vhi, vhi, vlo], axis=0)) * flip
    angle = (np.arange(lon)[:, None] * np.arange(KMAX)[None, :] % nlon) * (2.0 * math.pi / nlon)
    table = np.concatenate([np.cos(angle), np.sin(angle)], axis=1)
    thi, tlo = split_np(table)
    ihi, ilo = np.ascontiguousarray(thi.T), np.ascontiguousarray(tlo.T)

    def whole(x):
        return pl.BlockSpec(x.shape, lambda i: (0,) * x.ndim)

    def stage(*shape):
        return pl.BlockSpec((1,) + shape, lambda i: (i,) + (0,) * len(shape))

    band = pl.BlockSpec((nf, chunk, nlev, lon), lambda i: (0, i, 0, 0))
    before = pl.BlockSpec((nf, 1, nlev, lon), lambda i: (0, jnp.maximum(i * chunk - 1, 0), 0, 0))
    after = pl.BlockSpec((nf, 1, nlev, lon), lambda i: (0, jnp.minimum(i * chunk + chunk, rows - 1), 0, 0))
    m = nf * chunk * nlev
    params = pltpu.CompilerParams(vmem_limit_bytes=32 * 1024 * 1024)
    u = jnp.asarray(u)
    out = pl.pallas_call(
        functools.partial(first_kernel, ranks, 1.0 / (2.0 * dlon), 1.0 / (2.0 * dlat)),
        grid=(steps,),
        in_specs=[band, before, after, whole(low), whole(high)]
        + [stage(nlev, nf * chunk)] * 2
        + [stage(chunk + 2, nlev, 128), stage(chunk, wide), stage(chunk, wide), whole(u)],
        out_specs=[band] + [stage(2 * r, m) for r in ranks],
        out_shape=[jax.ShapeDtypeStruct(fields.shape, F32)]
        + [jax.ShapeDtypeStruct((steps, 2 * r, m), F32) for r in ranks],
        scratch_shapes=[pltpu.VMEM((nf, chunk + 2, nlev, wide), F32)],
        compiler_params=params,
        name="tendency",
    )(fields, fields, fields, low, high, east, west, cosine, cphase, sphase, u)
    tend, sent = out[0], out[1:]
    got = [around(h, off) for off, h in zip(range(1, lon_count), sent)]
    shared = [jnp.asarray(x) for x in (thi, tlo, ihi, ilo)] + [v]
    out = pl.pallas_call(
        functools.partial(second_kernel, ranks),
        grid=(steps,),
        in_specs=[band, band, stage(chunk, lon), stage(chunk, lon), stage(chunk, lon), stage(chunk, 2 * KMAX)]
        + [whole(x) for x in shared]
        + [stage(2 * r, m) for r in ranks],
        out_specs=band,
        out_shape=jax.ShapeDtypeStruct(fields.shape, F32),
        compiler_params=params,
        name="projection",
    )(fields, tend, con, son, keep, weights, *shared, *got)
    return jnp.transpose(out, (0, 2, 1, 3))


def solution(mesh):
    placed = (P(None, None, "lat", "lon"), P("lat"), P("lat"))
    return jax.shard_map(
        shards, mesh=mesh, in_specs=placed, out_specs=P(None, None, "lat", "lon"), check_vma=False
    )
```

```python
import functools
import math

import jax
import jax.numpy as jnp
import ml_dtypes
import numpy as np
from jax import lax
from jax.experimental import pallas as pl
from jax.experimental.pallas import tpu as pltpu
from jax.sharding import PartitionSpec as P

KMAX = 128
F32, BF16 = jnp.float32, jnp.bfloat16
MESH = pl.DeviceIdType.MESH
NT = (((1,), (1,)), ((), ()))
NN = (((1,), (0,)), ((), ()))
TN = (((0,), (0,)), ((), ()))


def split_np(a):
    hi = a.astype(ml_dtypes.bfloat16)
    lo = (a - hi.astype(np.float64)).astype(ml_dtypes.bfloat16)
    return hi, lo


def split(a):
    hi = a.astype(BF16)
    return hi, (a - hi.astype(F32)).astype(BF16)


def dot(a, b, dims):
    return lax.dot_general(a, b, dims, preferred_element_type=F32)


@functools.lru_cache(maxsize=None)
def factors(nlon, width):
    source, target, ranks = [], [], []
    for off in range(1, nlon // width):
        gaps = np.array(
            [1.0 / (nlon * math.sin((off * width + d) * math.pi / nlon)) for d in range(1 - width, width)]
        )
        idx = np.arange(width)
        rest = gaps[idx[:, None] - idx[None, :] + width - 1]
        bias = 1.0 + 1e-6 * idx[:, None] / width
        src, tgt = [], []
        while len(src) % 8 or not src or np.abs(rest).max() > 1e-9:
            i, j = np.unravel_index(np.argmax(np.abs(rest) * bias), rest.shape)
            row, col = rest[i] / rest[i, j], rest[:, j].copy()
            src.append(row)
            tgt.append(col)
            rest = rest - col[:, None] * row[None, :]
        ranks.append(len(src))
        source += src
        target += tgt
    return np.stack(source), np.stack(target), tuple(ranks)


def per_level(table, nlev):
    return jnp.concatenate(
        [jnp.broadcast_to(table[r : r + 1], (nlev, table.shape[1])) for r in range(table.shape[0])], axis=0
    )


def first_kernel(ranks, a, b, chunk, f_any, cos_ref, c_ref, s_ref, u_ref, t_ref, *rest):
    n_off = len(ranks)
    got, (fv, w, halo, edge, ghost), held = rest[:n_off], rest[n_off : n_off + 5], rest[n_off + 5 : 2 * n_off + 5]
    load_sem, row_send, row_recv, col_send, col_recv, far_send, far_recv = rest[2 * n_off + 5 :]
    nf, rows, nlev, lon = fv.shape
    wide = w.shape[3]
    steps = rows // chunk
    flat = (chunk * nlev, wide)
    lat_pos, lon_pos = lax.axis_index("lat"), lax.axis_index("lon")
    lats, lons = lax.axis_size("lat"), lax.axis_size("lon")
    opposite = lax.rem(lon_pos + lons // 2, lons)

    def peer(off):
        return lax.rem(lon_pos + off, lons)

    load = pltpu.make_async_copy(f_any, fv, load_sem)
    load.start()
    barrier = pltpu.get_barrier_semaphore()

    def greet(lat, lon_at):
        pl.semaphore_signal(barrier, inc=1, device_id=(lon_at, lat), device_id_type=MESH)

    for off in range(1, lons):
        greet(lat_pos, peer(off))

    @pl.when(lat_pos > 0)
    def _():
        greet(lat_pos - 1, lon_pos)

    @pl.when(lat_pos < lats - 1)
    def _():
        greet(lat_pos + 1, lon_pos)

    peers = lons - 1 + jnp.minimum(lat_pos, 1) + jnp.minimum(lats - 1 - lat_pos, 1)
    pl.semaphore_wait(barrier, peers)

    def row_copy(row, slot, lat, lon_at, which):
        return pltpu.make_async_remote_copy(
            src_ref=f_any.at[:, row],
            dst_ref=halo.at[slot],
            send_sem=row_send.at[which],
            recv_sem=row_recv.at[slot],
            device_id=(lon_at, lat),
            device_id_type=MESH,
        )

    @pl.when(lat_pos > 0)
    def _():
        row_copy(0, 1, lat_pos - 1, lon_pos, 0).start()

    @pl.when(lat_pos == 0)
    def _():
        row_copy(0, 0, lat_pos, opposite, 0).start()

    @pl.when(lat_pos < lats - 1)
    def _():
        row_copy(rows - 1, 0, lat_pos + 1, lon_pos, 1).start()

    @pl.when(lat_pos == lats - 1)
    def _():
        row_copy(rows - 1, 1, lat_pos, opposite, 1).start()

    w[:, :, :, lon:wide] = jnp.zeros((nf, chunk + 2, nlev, wide - lon), F32)
    lane = lax.broadcasted_iota(jnp.int32, (nlev, 128), 1)
    load.wait()

    def pack(i, carry):
        west_edge = jnp.zeros((nlev, 128), F32)
        east_edge = jnp.zeros((nlev, 128), F32)
        for f in range(nf):
            for r in range(chunk):
                here = lane == f * chunk + r
                west_edge = jnp.where(here, fv[f, i * chunk + r, :, 0:1], west_edge)
                east_edge = jnp.where(here, fv[f, i * chunk + r, :, lon - 1 : lon], east_edge)
        edge[0, i] = west_edge
        edge[1, i] = east_edge
        return carry

    lax.fori_loop(0, steps, pack, 0)
    cols = [
        pltpu.make_async_remote_copy(
            src_ref=edge.at[side],
            dst_ref=ghost.at[side],
            send_sem=col_send.at[side],
            recv_sem=col_recv.at[side],
            device_id=(peer(lons - 1 if side == 0 else 1), lat_pos),
            device_id_type=MESH,
        )
        for side in range(2)
    ]
    for copy in cols:
        copy.start()
    for which in range(2):
        row_copy(0, which, lat_pos, opposite, which).wait()
    for copy in cols:
        copy.wait()
    turn_low = jnp.where(lat_pos == 0, -1.0, 1.0)
    turn_high = jnp.where(lat_pos == lats - 1, -1.0, 1.0)

    def far_copy(at, i):
        return pltpu.make_async_remote_copy(
            src_ref=held[at].at[i],
            dst_ref=got[at].at[i],
            send_sem=far_send.at[at, i],
            recv_sem=far_recv.at[at, i],
            device_id=(peer(at + 1), lat_pos),
            device_id_type=MESH,
        )

    def dx(z):
        return pltpu.roll(z, wide - 1, 1) - pltpu.roll(z, 1, 1)

    def dy(z):
        return (z[2:] - z[:-2]).reshape(flat)

    def work(i, carry):
        for f in range(nf):
            below, above = halo[0, f], halo[1, f]
            if f in (1, 2):
                below, above = below * turn_low, above * turn_high
            w[f, 1 : chunk + 1, :, 0:lon] = fv[f, pl.ds(i * chunk, chunk)]
            w[f, 0, :, 0:lon] = jnp.where(i == 0, below, fv[f, jnp.maximum(i * chunk - 1, 0)])
            w[f, chunk + 1, :, 0:lon] = jnp.where(
                i == steps - 1, above, fv[f, jnp.minimum(i * chunk + chunk, rows - 1)]
            )
            for r in range(chunk):
                k = f * chunk + r
                w[f, r + 1, :, lon : lon + 1] = ghost[0, i, :, k : k + 1]
                w[f, r + 1, :, wide - 1 : wide] = ghost[1, i, :, k : k + 1]

        def mid(f):
            return w[f, 1 : chunk + 1].reshape(flat)

        ua = mid(1) * (-a)
        cv = w[2] * (cos_ref[i][:, :, 0:1] * (-b))
        tend = [dx(ua) + dy(cv), dx(mid(0)) * (-a), dy(w[0]) * (-b)]
        for f in range(3, nf):
            tend.append(dx(ua * mid(f)) + dy(cv * w[f]))
        parts = []
        for table in (per_level(c_ref[i], nlev), per_level(s_ref[i], nlev)):
            pairs = [split(t * table) for t in tend]
            hi = jnp.concatenate([p[0] for p in pairs], axis=0)
            lo = jnp.concatenate([p[1] for p in pairs], axis=0)
            n = u_ref.shape[0] // 2
            both = dot(u_ref[...], hi, NT)
            parts.append(both[:n] + both[n:] + dot(u_ref[0:n], lo, NT))
        at = 0
        for off, r in enumerate(ranks):
            held[off][i, 0:r] = parts[0][at : at + r]
            held[off][i, r : 2 * r] = parts[1][at : at + r]
            far_copy(off, i).start()
            at += r
        for f in range(nf):
            t_ref[f, pl.ds(i * chunk, chunk)] = tend[f][:, 0:lon].reshape(chunk, nlev, lon)
        return carry

    lax.fori_loop(0, steps, work, 0)

    def finish(i, carry):
        for off in range(n_off):
            far_copy(off, i).wait()
        return carry

    lax.fori_loop(0, steps, finish, 0)


def second_kernel(ranks, f_ref, t_ref, c_ref, s_ref, keep_ref, wt_ref, thi, tlo, ihi, ilo, v_ref, *rest):
    h_refs, o_ref = rest[:-1], rest[-1]
    nf, chunk, nlev, lon = f_ref.shape
    m = chunk * nlev
    tend = [t_ref[f].reshape(m, lon) for f in range(nf)]
    hi, lo = split(jnp.concatenate(tend, axis=0))
    spec = dot(hi, thi[...], NN) + dot(hi, tlo[...], NN) + dot(lo, thi[...], NN)
    wt = per_level(wt_ref[0], nlev)
    spec = jnp.concatenate([spec[f * m : (f + 1) * m] * wt for f in range(nf)], axis=0)
    hi, lo = split(spec)
    local = dot(hi, ihi[...], NN) + dot(hi, ilo[...], NN) + dot(lo, ihi[...], NN)
    far = []
    spare = v_ref.shape[0] // 3 - sum(ranks)
    for part in range(2):
        h = [ref[0, part * r : (part + 1) * r] for ref, r in zip(h_refs, ranks)]
        if spare:
            h.append(jnp.zeros((spare, nf * m), F32))
        hi, lo = split(jnp.concatenate(h, axis=0))
        far.append(dot(jnp.concatenate([hi, lo, hi], axis=0), v_ref[...], TN))
    c, s, keep = (per_level(x[0], nlev) for x in (c_ref, s_ref, keep_ref))
    for f in range(nf):
        at = slice(f * m, (f + 1) * m)
        add = local[at] + far[0][at] * s - far[1][at] * c + tend[f] * keep
        o_ref[f] = f_ref[f] + add.reshape(chunk, nlev, lon)


def shards(fields, mask, cutoff):
    fields = jnp.transpose(fields, (0, 2, 1, 3))
    nf, rows, nlev, lon = fields.shape
    chunk = max(c for c in range(1, 7) if rows % c == 0)
    steps = rows // chunk
    lon_count = lax.axis_size("lon")
    lat_count = lax.axis_size("lat")
    nlon, nlat = lon * lon_count, rows * lat_count
    dlon, dlat = 2.0 * math.pi / nlon, math.pi / nlat
    step = 0.4 * dlon
    lat_pos, lon_pos = lax.axis_index("lat"), lax.axis_index("lon")
    wide = -(-(lon + 2) // 128) * 128
    source, target, ranks = factors(nlon, lon)
    total = sum(ranks)
    padr = -(-total // 16) * 16

    rowid = np.arange(steps)[:, None] * chunk + np.arange(chunk + 2)[None, :] - 1
    rowid = jnp.clip(lat_pos * rows + rowid, 0, nlat - 1)
    cosine = jnp.cos(-math.pi / 2 + (rowid.astype(F32) + 0.5) * dlat)
    cosine = jnp.broadcast_to(cosine[:, :, None, None], (steps, chunk + 2, nlev, 128))
    cut = cutoff.reshape(steps, chunk)
    on = mask.astype(F32).reshape(steps, chunk) * step
    cols = lon_pos * lon + jnp.arange(wide, dtype=jnp.int32)
    turn = ((2 * cut[:, :, None] - 1) * cols) % (2 * nlon)
    phase = turn.astype(F32) * (math.pi / nlon)
    inside = (jnp.arange(wide) < lon).astype(F32)
    cphase, sphase = jnp.cos(phase) * inside, jnp.sin(phase) * inside
    con, son = cphase[:, :, :lon] * on[:, :, None], sphase[:, :, :lon] * on[:, :, None]
    keep = jnp.broadcast_to((step - on)[:, :, None], (steps, chunk, lon))
    wavenum = jnp.arange(KMAX)
    scale = jnp.where(wavenum == 0, 1.0 / nlon, 2.0 / nlon).astype(F32)
    weights = (wavenum < cut[:, :, None]).astype(F32) * scale * on[:, :, None]
    weights = jnp.concatenate([weights, weights], axis=2)

    u = np.zeros((padr, wide))
    u[:total, :lon] = source
    u = np.concatenate(split_np(u), axis=0)
    v = np.zeros((padr, lon))
    v[:total] = target
    vhi, vlo = split_np(v)
    flip, at = [], 0
    for off, r in zip(range(1, lon_count), ranks):
        flip.append(jnp.where(lon_pos >= off, 1.0, -1.0) * jnp.ones((r,)))
    flip = jnp.concatenate(flip + [jnp.ones((padr - total,))])
    flip = jnp.concatenate([flip] * 3).astype(BF16)[:, None]
    v = jnp.asarray(np.concatenate([vhi, vhi, vlo], axis=0)) * flip
    angle = (np.arange(lon)[:, None] * np.arange(KMAX)[None, :] % nlon) * (2.0 * math.pi / nlon)
    table = np.concatenate([np.cos(angle), np.sin(angle)], axis=1)
    thi, tlo = split_np(table)
    ihi, ilo = np.ascontiguousarray(thi.T), np.ascontiguousarray(tlo.T)

    def whole(x):
        return pl.BlockSpec(x.shape, lambda i: (0,) * x.ndim)

    def stage(*shape):
        return pl.BlockSpec((1,) + shape, lambda i: (i,) + (0,) * len(shape))

    band = pl.BlockSpec((nf, chunk, nlev, lon), lambda i: (0, i, 0, 0))
    m = nf * chunk * nlev
    params = pltpu.CompilerParams(vmem_limit_bytes=32 * 1024 * 1024)
    u = jnp.asarray(u)
    n_off = len(ranks)
    vmem, far = pl.BlockSpec(memory_space=pltpu.VMEM), pl.BlockSpec(memory_space=pl.ANY)
    out = pl.pallas_call(
        functools.partial(first_kernel, ranks, 1.0 / (2.0 * dlon), 1.0 / (2.0 * dlat), chunk),
        in_specs=[far] + [vmem] * 4,
        out_specs=[vmem] + [far] * n_off,
        out_shape=[jax.ShapeDtypeStruct(fields.shape, F32)]
        + [jax.ShapeDtypeStruct((steps, 2 * r, m), F32) for r in ranks],
        scratch_shapes=[
            pltpu.VMEM(fields.shape, F32),
            pltpu.VMEM((nf, chunk + 2, nlev, wide), F32),
            pltpu.VMEM((2, nf, nlev, lon), F32),
            pltpu.VMEM((2, steps, nlev, 128), F32),
            pltpu.VMEM((2, steps, nlev, 128), F32),
        ]
        + [pltpu.VMEM((steps, 2 * r, m), F32) for r in ranks]
        + [
            pltpu.SemaphoreType.DMA,
            pltpu.SemaphoreType.DMA((2,)),
            pltpu.SemaphoreType.DMA((2,)),
            pltpu.SemaphoreType.DMA((2,)),
            pltpu.SemaphoreType.DMA((2,)),
            pltpu.SemaphoreType.DMA((n_off, steps)),
            pltpu.SemaphoreType.DMA((n_off, steps)),
        ],
        compiler_params=pltpu.CompilerParams(
            vmem_limit_bytes=48 * 1024 * 1024, collective_id=0, has_side_effects=True
        ),
        name="tendency",
    )(fields, cosine, cphase, sphase, u)
    tend, got = out[0], out[1:]
    shared = [jnp.asarray(x) for x in (thi, tlo, ihi, ilo)] + [v]
    out = pl.pallas_call(
        functools.partial(second_kernel, ranks),
        grid=(steps,),
        in_specs=[band, band, stage(chunk, lon), stage(chunk, lon), stage(chunk, lon), stage(chunk, 2 * KMAX)]
        + [whole(x) for x in shared]
        + [stage(2 * r, m) for r in ranks],
        out_specs=band,
        out_shape=jax.ShapeDtypeStruct(fields.shape, F32),
        compiler_params=params,
        name="projection",
    )(fields, tend, con, son, keep, weights, *shared, *got)
    return jnp.transpose(out, (0, 2, 1, 3))


def solution(mesh):
    placed = (P(None, None, "lat", "lon"), P("lat"), P("lat"))
    return jax.shard_map(
        shards, mesh=mesh, in_specs=placed, out_specs=P(None, None, "lat", "lon"), check_vma=False
    )
```

```python
import functools
import math

import jax
import jax.numpy as jnp
import ml_dtypes
import numpy as np
from jax import lax
from jax.experimental import pallas as pl
from jax.experimental.pallas import tpu as pltpu
from jax.sharding import PartitionSpec as P

KMAX = 128
F32, BF16 = jnp.float32, jnp.bfloat16
MESH = pl.DeviceIdType.MESH
NT = (((1,), (1,)), ((), ()))
NN = (((1,), (0,)), ((), ()))
TN = (((0,), (0,)), ((), ()))


def split_np(a):
    hi = a.astype(ml_dtypes.bfloat16)
    lo = (a - hi.astype(np.float64)).astype(ml_dtypes.bfloat16)
    return hi, lo


def split(a):
    hi = a.astype(BF16)
    return hi, (a - hi.astype(F32)).astype(BF16)


def dot(a, b, dims):
    return lax.dot_general(a, b, dims, preferred_element_type=F32)


@functools.lru_cache(maxsize=None)
def factors(nlon, width):
    source, target, ranks = [], [], []
    for off in range(1, nlon // width):
        gaps = np.array(
            [1.0 / (nlon * math.sin((off * width + d) * math.pi / nlon)) for d in range(1 - width, width)]
        )
        idx = np.arange(width)
        rest = gaps[idx[:, None] - idx[None, :] + width - 1]
        bias = 1.0 + 1e-6 * idx[:, None] / width
        src, tgt = [], []
        while len(src) % 8 or not src or np.abs(rest).max() > 1e-9:
            i, j = np.unravel_index(np.argmax(np.abs(rest) * bias), rest.shape)
            row, col = rest[i] / rest[i, j], rest[:, j].copy()
            src.append(row)
            tgt.append(col)
            rest = rest - col[:, None] * row[None, :]
        ranks.append(len(src))
        source += src
        target += tgt
    return np.stack(source), np.stack(target), tuple(ranks)


def per_level(table, nlev):
    return jnp.concatenate(
        [jnp.broadcast_to(table[r : r + 1], (nlev, table.shape[1])) for r in range(table.shape[0])], axis=0
    )


def polar(lat_pos, lats, rows, chunk, i):
    nlat = lats * rows
    start = lat_pos * rows + i * chunk
    return (start < nlat // 6) | (start + chunk > nlat - nlat // 6)


def first_kernel(
    ranks, a, b, chunk, f_any, cos_ref, c_ref, s_ref, u_ref, keep_ref, wt_ref, thi, tlo, ihi, ilo, t_ref, *rest
):
    n_off = len(ranks)
    got, (fv, w, halo, edge, ghost), held = rest[:n_off], rest[n_off : n_off + 5], rest[n_off + 5 : 2 * n_off + 5]
    load_sem, row_send, row_recv, col_send, col_recv, far_send, far_recv = rest[2 * n_off + 5 :]
    nf, rows, nlev, lon = fv.shape
    wide = w.shape[3]
    steps = rows // chunk
    flat = (chunk * nlev, wide)
    lat_pos, lon_pos = lax.axis_index("lat"), lax.axis_index("lon")
    lats, lons = lax.axis_size("lat"), lax.axis_size("lon")
    opposite = lax.rem(lon_pos + lons // 2, lons)

    def peer(off):
        return lax.rem(lon_pos + off, lons)

    load = pltpu.make_async_copy(f_any, fv, load_sem)
    load.start()
    barrier = pltpu.get_barrier_semaphore()

    def greet(lat, lon_at):
        pl.semaphore_signal(barrier, inc=1, device_id=(lon_at, lat), device_id_type=MESH)

    for off in range(1, lons):
        greet(lat_pos, peer(off))

    @pl.when(lat_pos > 0)
    def _():
        greet(lat_pos - 1, lon_pos)

    @pl.when(lat_pos < lats - 1)
    def _():
        greet(lat_pos + 1, lon_pos)

    peers = lons - 1 + jnp.minimum(lat_pos, 1) + jnp.minimum(lats - 1 - lat_pos, 1)
    pl.semaphore_wait(barrier, peers)

    def row_copy(row, slot, lat, lon_at, which):
        return pltpu.make_async_remote_copy(
            src_ref=f_any.at[:, row],
            dst_ref=halo.at[slot],
            send_sem=row_send.at[which],
            recv_sem=row_recv.at[slot],
            device_id=(lon_at, lat),
            device_id_type=MESH,
        )

    @pl.when(lat_pos > 0)
    def _():
        row_copy(0, 1, lat_pos - 1, lon_pos, 0).start()

    @pl.when(lat_pos == 0)
    def _():
        row_copy(0, 0, lat_pos, opposite, 0).start()

    @pl.when(lat_pos < lats - 1)
    def _():
        row_copy(rows - 1, 0, lat_pos + 1, lon_pos, 1).start()

    @pl.when(lat_pos == lats - 1)
    def _():
        row_copy(rows - 1, 1, lat_pos, opposite, 1).start()

    w[:, :, :, lon:wide] = jnp.zeros((nf, chunk + 2, nlev, wide - lon), F32)
    lane = lax.broadcasted_iota(jnp.int32, (nlev, 128), 1)
    load.wait()

    def pack(i, carry):
        west_edge = jnp.zeros((nlev, 128), F32)
        east_edge = jnp.zeros((nlev, 128), F32)
        for f in range(nf):
            for r in range(chunk):
                here = lane == f * chunk + r
                west_edge = jnp.where(here, fv[f, i * chunk + r, :, 0:1], west_edge)
                east_edge = jnp.where(here, fv[f, i * chunk + r, :, lon - 1 : lon], east_edge)
        edge[0, i] = west_edge
        edge[1, i] = east_edge
        return carry

    lax.fori_loop(0, steps, pack, 0)
    cols = [
        pltpu.make_async_remote_copy(
            src_ref=edge.at[side],
            dst_ref=ghost.at[side],
            send_sem=col_send.at[side],
            recv_sem=col_recv.at[side],
            device_id=(peer(lons - 1 if side == 0 else 1), lat_pos),
            device_id_type=MESH,
        )
        for side in range(2)
    ]
    for copy in cols:
        copy.start()
    for which in range(2):
        row_copy(0, which, lat_pos, opposite, which).wait()
    for copy in cols:
        copy.wait()
    turn_low = jnp.where(lat_pos == 0, -1.0, 1.0)
    turn_high = jnp.where(lat_pos == lats - 1, -1.0, 1.0)

    def far_copy(at, i):
        return pltpu.make_async_remote_copy(
            src_ref=held[at].at[i],
            dst_ref=got[at].at[i],
            send_sem=far_send.at[at, i],
            recv_sem=far_recv.at[at, i],
            device_id=(peer(at + 1), lat_pos),
            device_id_type=MESH,
        )

    def dx(z):
        return pltpu.roll(z, wide - 1, 1) - pltpu.roll(z, 1, 1)

    def dy(z):
        return (z[2:] - z[:-2]).reshape(flat)

    def work(i, carry):
        for f in range(nf):
            below, above = halo[0, f], halo[1, f]
            if f in (1, 2):
                below, above = below * turn_low, above * turn_high
            w[f, 1 : chunk + 1, :, 0:lon] = fv[f, pl.ds(i * chunk, chunk)]
            w[f, 0, :, 0:lon] = jnp.where(i == 0, below, fv[f, jnp.maximum(i * chunk - 1, 0)])
            w[f, chunk + 1, :, 0:lon] = jnp.where(
                i == steps - 1, above, fv[f, jnp.minimum(i * chunk + chunk, rows - 1)]
            )
            for r in range(chunk):
                k = f * chunk + r
                w[f, r + 1, :, lon : lon + 1] = ghost[0, i, :, k : k + 1]
                w[f, r + 1, :, wide - 1 : wide] = ghost[1, i, :, k : k + 1]

        def mid(f):
            return w[f, 1 : chunk + 1].reshape(flat)

        ua = mid(1) * (-a)
        cv = w[2] * (cos_ref[i][:, :, 0:1] * (-b))
        tend = [dx(ua) + dy(cv), dx(mid(0)) * (-a), dy(w[0]) * (-b)]
        for f in range(3, nf):
            tend.append(dx(ua * mid(f)) + dy(cv * w[f]))
        parts = []
        for table in (per_level(c_ref[i], nlev), per_level(s_ref[i], nlev)):
            pairs = [split(t * table) for t in tend]
            hi = jnp.concatenate([p[0] for p in pairs], axis=0)
            lo = jnp.concatenate([p[1] for p in pairs], axis=0)
            n = u_ref.shape[0] // 2
            both = dot(u_ref[...], hi, NT)
            parts.append(both[:n] + both[n:] + dot(u_ref[0:n], lo, NT))
        at = 0
        for off, r in enumerate(ranks):
            turned = jnp.where(lon_pos + off + 1 >= lons, -1.0, 1.0)
            held[off][i, 0:r] = parts[0][at : at + r] * turned
            held[off][i, r : 2 * r] = parts[1][at : at + r] * turned
            at += r

        @pl.when(polar(lat_pos, lats, rows, chunk, i))
        def _():
            for off in range(n_off):
                far_copy(off, i).start()

        for f in range(nf):
            t_ref[f, pl.ds(i * chunk, chunk)] = tend[f][:, 0:lon].reshape(chunk, nlev, lon)
        return carry

    lax.fori_loop(0, steps, work, 0)

    def local(i, carry):
        m = chunk * nlev
        tend = [t_ref[f, pl.ds(i * chunk, chunk)].reshape(m, lon) for f in range(nf)]
        hi, lo = split(jnp.concatenate(tend, axis=0))
        spec = dot(hi, thi[...], NN) + dot(hi, tlo[...], NN) + dot(lo, thi[...], NN)
        wt = per_level(wt_ref[i], nlev)
        spec = jnp.concatenate([spec[f * m : (f + 1) * m] * wt for f in range(nf)], axis=0)
        hi, lo = split(spec)
        proj = dot(hi, ihi[...], NN) + dot(hi, ilo[...], NN) + dot(lo, ihi[...], NN)
        keep = per_level(keep_ref[i], nlev)
        for f in range(nf):
            add = proj[f * m : (f + 1) * m] + tend[f] * keep
            t_ref[f, pl.ds(i * chunk, chunk)] = fv[f, pl.ds(i * chunk, chunk)] + add.reshape(chunk, nlev, lon)
        return carry

    lax.fori_loop(0, steps, local, 0)

    def finish(i, carry):
        @pl.when(polar(lat_pos, lats, rows, chunk, i))
        def _():
            for off in range(n_off):
                far_copy(off, i).wait()

        return carry

    lax.fori_loop(0, steps, finish, 0)


def second_kernel(ranks, on_ref, t_ref, c_ref, s_ref, v_ref, *rest):
    h_refs, o_ref = rest[:-1], rest[-1]
    nf, chunk, nlev, lon = t_ref.shape
    m = chunk * nlev
    active = on_ref[pl.program_id(0)] != 0

    @pl.when(active)
    def _():
        far = []
        spare = v_ref.shape[0] // 3 - sum(ranks)
        for part in range(2):
            h = [ref[0, part * r : (part + 1) * r] for ref, r in zip(h_refs, ranks)]
            if spare:
                h.append(jnp.zeros((spare, nf * m), F32))
            hi, lo = split(jnp.concatenate(h, axis=0))
            far.append(dot(jnp.concatenate([hi, lo, hi], axis=0), v_ref[...], TN))
        c, s = (per_level(x[0], nlev) for x in (c_ref, s_ref))
        for f in range(nf):
            at = slice(f * m, (f + 1) * m)
            o_ref[f] = t_ref[f] + (far[0][at] * s - far[1][at] * c).reshape(chunk, nlev, lon)

    @pl.when(jnp.logical_not(active))
    def _():
        o_ref[...] = t_ref[...]


def shards(fields, mask, cutoff):
    fields = jnp.transpose(fields, (0, 2, 1, 3))
    nf, rows, nlev, lon = fields.shape
    chunk = max(c for c in range(1, 7) if rows % c == 0)
    steps = rows // chunk
    lon_count = lax.axis_size("lon")
    lat_count = lax.axis_size("lat")
    nlon, nlat = lon * lon_count, rows * lat_count
    dlon, dlat = 2.0 * math.pi / nlon, math.pi / nlat
    step = 0.4 * dlon
    lat_pos, lon_pos = lax.axis_index("lat"), lax.axis_index("lon")
    wide = -(-(lon + 2) // 128) * 128
    source, target, ranks = factors(nlon, lon)
    total = sum(ranks)
    padr = -(-total // 16) * 16

    rowid = np.arange(steps)[:, None] * chunk + np.arange(chunk + 2)[None, :] - 1
    rowid = jnp.clip(lat_pos * rows + rowid, 0, nlat - 1)
    cosine = jnp.cos(-math.pi / 2 + (rowid.astype(F32) + 0.5) * dlat)
    cosine = jnp.broadcast_to(cosine[:, :, None, None], (steps, chunk + 2, nlev, 128))
    cut = cutoff.reshape(steps, chunk)
    on = mask.astype(F32).reshape(steps, chunk) * step
    cols = lon_pos * lon + jnp.arange(wide, dtype=jnp.int32)
    turn = ((2 * cut[:, :, None] - 1) * cols) % (2 * nlon)
    phase = turn.astype(F32) * (math.pi / nlon)
    inside = (jnp.arange(wide) < lon).astype(F32)
    cphase, sphase = jnp.cos(phase) * inside, jnp.sin(phase) * inside
    con, son = cphase[:, :, :lon] * on[:, :, None], sphase[:, :, :lon] * on[:, :, None]
    keep = jnp.broadcast_to((step - on)[:, :, None], (steps, chunk, lon))
    wavenum = jnp.arange(KMAX)
    scale = jnp.where(wavenum == 0, 1.0 / nlon, 2.0 / nlon).astype(F32)
    weights = (wavenum < cut[:, :, None]).astype(F32) * scale * on[:, :, None]
    weights = jnp.concatenate([weights, weights], axis=2)

    u = np.zeros((padr, wide))
    u[:total, :lon] = source
    u = np.concatenate(split_np(u), axis=0)
    v = np.zeros((padr, lon))
    v[:total] = target
    vhi, vlo = split_np(v)
    v = jnp.asarray(np.concatenate([vhi, vhi, vlo], axis=0))
    angle = (np.arange(lon)[:, None] * np.arange(KMAX)[None, :] % nlon) * (2.0 * math.pi / nlon)
    table = np.concatenate([np.cos(angle), np.sin(angle)], axis=1)
    thi, tlo = split_np(table)
    ihi, ilo = np.ascontiguousarray(thi.T), np.ascontiguousarray(tlo.T)

    def whole(x):
        return pl.BlockSpec(x.shape, lambda i: (0,) * x.ndim)

    def stage(*shape):
        return pl.BlockSpec((1,) + shape, lambda i: (i,) + (0,) * len(shape))

    band = pl.BlockSpec((nf, chunk, nlev, lon), lambda i: (0, i, 0, 0))
    m = nf * chunk * nlev
    params = pltpu.CompilerParams(vmem_limit_bytes=32 * 1024 * 1024)
    u = jnp.asarray(u)
    tables = [jnp.asarray(x) for x in (thi, tlo, ihi, ilo)]
    n_off = len(ranks)
    vmem, far = pl.BlockSpec(memory_space=pltpu.VMEM), pl.BlockSpec(memory_space=pl.ANY)
    out = pl.pallas_call(
        functools.partial(first_kernel, ranks, 1.0 / (2.0 * dlon), 1.0 / (2.0 * dlat), chunk),
        in_specs=[far] + [vmem] * 10,
        out_specs=[vmem] + [far] * n_off,
        out_shape=[jax.ShapeDtypeStruct(fields.shape, F32)]
        + [jax.ShapeDtypeStruct((steps, 2 * r, m), F32) for r in ranks],
        scratch_shapes=[
            pltpu.VMEM(fields.shape, F32),
            pltpu.VMEM((nf, chunk + 2, nlev, wide), F32),
            pltpu.VMEM((2, nf, nlev, lon), F32),
            pltpu.VMEM((2, steps, nlev, 128), F32),
            pltpu.VMEM((2, steps, nlev, 128), F32),
        ]
        + [pltpu.VMEM((steps, 2 * r, m), F32) for r in ranks]
        + [
            pltpu.SemaphoreType.DMA,
            pltpu.SemaphoreType.DMA((2,)),
            pltpu.SemaphoreType.DMA((2,)),
            pltpu.SemaphoreType.DMA((2,)),
            pltpu.SemaphoreType.DMA((2,)),
            pltpu.SemaphoreType.DMA((n_off, steps)),
            pltpu.SemaphoreType.DMA((n_off, steps)),
        ],
        compiler_params=pltpu.CompilerParams(
            vmem_limit_bytes=48 * 1024 * 1024, collective_id=0, has_side_effects=True
        ),
        name="tendency",
    )(fields, cosine, cphase, sphase, u, keep, weights, *tables)
    tend, got = out[0], out[1:]
    active = polar(lat_pos, lat_count, rows, chunk, jnp.arange(steps)).astype(jnp.int32)
    out = pl.pallas_call(
        functools.partial(second_kernel, ranks),
        grid=(steps,),
        in_specs=[pl.BlockSpec(memory_space=pltpu.SMEM), band, stage(chunk, lon), stage(chunk, lon), whole(v)]
        + [stage(2 * r, m) for r in ranks],
        out_specs=band,
        out_shape=jax.ShapeDtypeStruct(fields.shape, F32),
        compiler_params=params,
        name="projection",
    )(active, tend, con, son, v, *got)
    return jnp.transpose(out, (0, 2, 1, 3))


def solution(mesh):
    placed = (P(None, None, "lat", "lon"), P("lat"), P("lat"))
    return jax.shard_map(
        shards, mesh=mesh, in_specs=placed, out_specs=P(None, None, "lat", "lon"), check_vma=False
    )
```

```python
import functools
import math

import jax
import jax.numpy as jnp
import ml_dtypes
import numpy as np
from jax import lax
from jax.experimental import pallas as pl
from jax.experimental.pallas import tpu as pltpu
from jax.sharding import PartitionSpec as P

KMAX = 128
F32, BF16 = jnp.float32, jnp.bfloat16
MESH = pl.DeviceIdType.MESH
NT = (((1,), (1,)), ((), ()))
NN = (((1,), (0,)), ((), ()))
TN = (((0,), (0,)), ((), ()))


def split_np(a):
    hi = a.astype(ml_dtypes.bfloat16)
    lo = (a - hi.astype(np.float64)).astype(ml_dtypes.bfloat16)
    return hi, lo


def split(a):
    hi = a.astype(BF16)
    return hi, (a - hi.astype(F32)).astype(BF16)


def dot(a, b, dims):
    return lax.dot_general(a, b, dims, preferred_element_type=F32)


@functools.lru_cache(maxsize=None)
def factors(nlon, width):
    source, target, ranks = [], [], []
    for off in range(1, nlon // width):
        gaps = np.array(
            [1.0 / (nlon * math.sin((off * width + d) * math.pi / nlon)) for d in range(1 - width, width)]
        )
        idx = np.arange(width)
        rest = gaps[idx[:, None] - idx[None, :] + width - 1]
        bias = 1.0 + 1e-6 * idx[:, None] / width
        src, tgt = [], []
        while len(src) % 8 or not src or np.abs(rest).max() > 1e-9:
            i, j = np.unravel_index(np.argmax(np.abs(rest) * bias), rest.shape)
            row, col = rest[i] / rest[i, j], rest[:, j].copy()
            src.append(row)
            tgt.append(col)
            rest = rest - col[:, None] * row[None, :]
        ranks.append(len(src))
        source += src
        target += tgt
    return np.stack(source), np.stack(target), tuple(ranks)


def per_level(table, nlev):
    return jnp.concatenate(
        [jnp.broadcast_to(table[r : r + 1], (nlev, table.shape[1])) for r in range(table.shape[0])], axis=0
    )


def polar(lat_pos, lats, rows, chunk, i):
    nlat = lats * rows
    start = lat_pos * rows + i * chunk
    return (start < nlat // 6) | (start + chunk > nlat - nlat // 6)


def first_kernel(
    ranks, a, b, chunk, f_any, cos_ref, c_ref, s_ref, keep_ref, wt_ref, *rest
):
    tables_any, t_any, rest = rest[:5], rest[5], rest[6:]
    u_ref, thi, tlo, ihi, ilo = tables = rest[-8:-3]
    table_sem, t_ref, out_sem = rest[-3:]
    rest = rest[:-8]
    n_off = len(ranks)
    got, (fv, w, halo, edge, ghost), held = rest[:n_off], rest[n_off : n_off + 5], rest[n_off + 5 : 2 * n_off + 5]
    load_sem, row_send, row_recv, col_send, col_recv, far_send, far_recv = rest[2 * n_off + 5 :]
    nf, rows, nlev, lon = fv.shape
    wide = w.shape[3]
    steps = rows // chunk
    flat = (chunk * nlev, wide)
    lat_pos, lon_pos = lax.axis_index("lat"), lax.axis_index("lon")
    lats, lons = lax.axis_size("lat"), lax.axis_size("lon")
    opposite = lax.rem(lon_pos + lons // 2, lons)

    def peer(off):
        return lax.rem(lon_pos + off, lons)

    load = pltpu.make_async_copy(f_any, fv, load_sem)
    load.start()
    moves = [pltpu.make_async_copy(x, y, table_sem.at[n]) for n, (x, y) in enumerate(zip(tables_any, tables))]
    for move in moves:
        move.start()
    barrier = pltpu.get_barrier_semaphore()

    def greet(lat, lon_at):
        pl.semaphore_signal(barrier, inc=1, device_id=(lon_at, lat), device_id_type=MESH)

    for off in range(1, lons):
        greet(lat_pos, peer(off))

    @pl.when(lat_pos > 0)
    def _():
        greet(lat_pos - 1, lon_pos)

    @pl.when(lat_pos < lats - 1)
    def _():
        greet(lat_pos + 1, lon_pos)

    peers = lons - 1 + jnp.minimum(lat_pos, 1) + jnp.minimum(lats - 1 - lat_pos, 1)
    pl.semaphore_wait(barrier, peers)

    def row_copy(row, slot, lat, lon_at, which):
        return pltpu.make_async_remote_copy(
            src_ref=f_any.at[:, row],
            dst_ref=halo.at[slot],
            send_sem=row_send.at[which],
            recv_sem=row_recv.at[slot],
            device_id=(lon_at, lat),
            device_id_type=MESH,
        )

    @pl.when(lat_pos > 0)
    def _():
        row_copy(0, 1, lat_pos - 1, lon_pos, 0).start()

    @pl.when(lat_pos == 0)
    def _():
        row_copy(0, 0, lat_pos, opposite, 0).start()

    @pl.when(lat_pos < lats - 1)
    def _():
        row_copy(rows - 1, 0, lat_pos + 1, lon_pos, 1).start()

    @pl.when(lat_pos == lats - 1)
    def _():
        row_copy(rows - 1, 1, lat_pos, opposite, 1).start()

    w[:, :, :, lon:wide] = jnp.zeros((nf, chunk + 2, nlev, wide - lon), F32)
    lane = lax.broadcasted_iota(jnp.int32, (nlev, 128), 1)
    load.wait()

    def pack(i, carry):
        west_edge = jnp.zeros((nlev, 128), F32)
        east_edge = jnp.zeros((nlev, 128), F32)
        for f in range(nf):
            for r in range(chunk):
                here = lane == f * chunk + r
                west_edge = jnp.where(here, fv[f, i * chunk + r, :, 0:1], west_edge)
                east_edge = jnp.where(here, fv[f, i * chunk + r, :, lon - 1 : lon], east_edge)
        edge[0, i] = west_edge
        edge[1, i] = east_edge
        return carry

    lax.fori_loop(0, steps, pack, 0)
    cols = [
        pltpu.make_async_remote_copy(
            src_ref=edge.at[side],
            dst_ref=ghost.at[side],
            send_sem=col_send.at[side],
            recv_sem=col_recv.at[side],
            device_id=(peer(lons - 1 if side == 0 else 1), lat_pos),
            device_id_type=MESH,
        )
        for side in range(2)
    ]
    for copy in cols:
        copy.start()
    for which in range(2):
        row_copy(0, which, lat_pos, opposite, which).wait()
    for copy in cols:
        copy.wait()
    for move in moves:
        move.wait()
    turn_low = jnp.where(lat_pos == 0, -1.0, 1.0)
    turn_high = jnp.where(lat_pos == lats - 1, -1.0, 1.0)

    def far_copy(at, i):
        return pltpu.make_async_remote_copy(
            src_ref=held[at].at[i],
            dst_ref=got[at].at[i],
            send_sem=far_send.at[at, i],
            recv_sem=far_recv.at[at, i],
            device_id=(peer(at + 1), lat_pos),
            device_id_type=MESH,
        )

    def dx(z):
        return pltpu.roll(z, wide - 1, 1) - pltpu.roll(z, 1, 1)

    def dy(z):
        return (z[2:] - z[:-2]).reshape(flat)

    def work(i, carry):
        for f in range(nf):
            below, above = halo[0, f], halo[1, f]
            if f in (1, 2):
                below, above = below * turn_low, above * turn_high
            w[f, 1 : chunk + 1, :, 0:lon] = fv[f, pl.ds(i * chunk, chunk)]
            w[f, 0, :, 0:lon] = jnp.where(i == 0, below, fv[f, jnp.maximum(i * chunk - 1, 0)])
            w[f, chunk + 1, :, 0:lon] = jnp.where(
                i == steps - 1, above, fv[f, jnp.minimum(i * chunk + chunk, rows - 1)]
            )
            for r in range(chunk):
                k = f * chunk + r
                w[f, r + 1, :, lon : lon + 1] = ghost[0, i, :, k : k + 1]
                w[f, r + 1, :, wide - 1 : wide] = ghost[1, i, :, k : k + 1]

        def mid(f):
            return w[f, 1 : chunk + 1].reshape(flat)

        ua = mid(1) * (-a)
        cv = w[2] * (cos_ref[i][:, :, 0:1] * (-b))
        tend = [dx(ua) + dy(cv), dx(mid(0)) * (-a), dy(w[0]) * (-b)]
        for f in range(3, nf):
            tend.append(dx(ua * mid(f)) + dy(cv * w[f]))
        parts = []
        for table in (per_level(c_ref[i], nlev), per_level(s_ref[i], nlev)):
            pairs = [split(t * table) for t in tend]
            hi = jnp.concatenate([p[0] for p in pairs], axis=0)
            lo = jnp.concatenate([p[1] for p in pairs], axis=0)
            n = u_ref.shape[0] // 2
            both = dot(u_ref[...], hi, NT)
            parts.append(both[:n] + both[n:] + dot(u_ref[0:n], lo, NT))
        at = 0
        for off, r in enumerate(ranks):
            turned = jnp.where(lon_pos + off + 1 >= lons, -1.0, 1.0)
            held[off][i, 0:r] = parts[0][at : at + r] * turned
            held[off][i, r : 2 * r] = parts[1][at : at + r] * turned
            at += r

        @pl.when(polar(lat_pos, lats, rows, chunk, i))
        def _():
            for off in range(n_off):
                far_copy(off, i).start()

        for f in range(nf):
            t_ref[f, pl.ds(i * chunk, chunk)] = tend[f][:, 0:lon].reshape(chunk, nlev, lon)
        return carry

    lax.fori_loop(0, steps, work, 0)

    def out_copy(i):
        at = pl.ds(i * chunk, chunk)
        return pltpu.make_async_copy(t_ref.at[:, at], t_any.at[:, at], out_sem.at[i])

    def local(i, carry):
        m = chunk * nlev
        tend = [t_ref[f, pl.ds(i * chunk, chunk)].reshape(m, lon) for f in range(nf)]
        hi, lo = split(jnp.concatenate(tend, axis=0))
        spec = dot(hi, thi[...], NN) + dot(hi, tlo[...], NN) + dot(lo, thi[...], NN)
        wt = per_level(wt_ref[i], nlev)
        spec = jnp.concatenate([spec[f * m : (f + 1) * m] * wt for f in range(nf)], axis=0)
        hi, lo = split(spec)
        proj = dot(hi, ihi[...], NN) + dot(hi, ilo[...], NN) + dot(lo, ihi[...], NN)
        keep = per_level(keep_ref[i], nlev)
        for f in range(nf):
            add = proj[f * m : (f + 1) * m] + tend[f] * keep
            t_ref[f, pl.ds(i * chunk, chunk)] = fv[f, pl.ds(i * chunk, chunk)] + add.reshape(chunk, nlev, lon)
        out_copy(i).start()
        return carry

    lax.fori_loop(0, steps, local, 0)

    def finish(i, carry):
        out_copy(i).wait()

        @pl.when(polar(lat_pos, lats, rows, chunk, i))
        def _():
            for off in range(n_off):
                far_copy(off, i).wait()

        return carry

    lax.fori_loop(0, steps, finish, 0)


def second_kernel(ranks, on_ref, t_ref, c_ref, s_ref, v_ref, *rest):
    h_refs, o_ref = rest[:-1], rest[-1]
    nf, chunk, nlev, lon = t_ref.shape
    m = chunk * nlev
    active = on_ref[pl.program_id(0)] != 0

    @pl.when(active)
    def _():
        far = []
        spare = v_ref.shape[0] // 3 - sum(ranks)
        for part in range(2):
            h = [ref[0, part * r : (part + 1) * r] for ref, r in zip(h_refs, ranks)]
            if spare:
                h.append(jnp.zeros((spare, nf * m), F32))
            hi, lo = split(jnp.concatenate(h, axis=0))
            far.append(dot(jnp.concatenate([hi, lo, hi], axis=0), v_ref[...], TN))
        c, s = (per_level(x[0], nlev) for x in (c_ref, s_ref))
        for f in range(nf):
            at = slice(f * m, (f + 1) * m)
            o_ref[f] = t_ref[f] + (far[0][at] * s - far[1][at] * c).reshape(chunk, nlev, lon)

    @pl.when(jnp.logical_not(active))
    def _():
        o_ref[...] = t_ref[...]


def shards(fields, mask, cutoff):
    fields = jnp.transpose(fields, (0, 2, 1, 3))
    nf, rows, nlev, lon = fields.shape
    chunk = max(c for c in range(1, 7) if rows % c == 0)
    steps = rows // chunk
    lon_count = lax.axis_size("lon")
    lat_count = lax.axis_size("lat")
    nlon, nlat = lon * lon_count, rows * lat_count
    dlon, dlat = 2.0 * math.pi / nlon, math.pi / nlat
    step = 0.4 * dlon
    lat_pos, lon_pos = lax.axis_index("lat"), lax.axis_index("lon")
    wide = -(-(lon + 2) // 128) * 128
    source, target, ranks = factors(nlon, lon)
    total = sum(ranks)
    padr = -(-total // 16) * 16

    rowid = np.arange(steps)[:, None] * chunk + np.arange(chunk + 2)[None, :] - 1
    rowid = jnp.clip(lat_pos * rows + rowid, 0, nlat - 1)
    cosine = jnp.cos(-math.pi / 2 + (rowid.astype(F32) + 0.5) * dlat)
    cosine = jnp.broadcast_to(cosine[:, :, None, None], (steps, chunk + 2, nlev, 128))
    cut = cutoff.reshape(steps, chunk)
    on = mask.astype(F32).reshape(steps, chunk) * step
    cols = lon_pos * lon + jnp.arange(wide, dtype=jnp.int32)
    turn = ((2 * cut[:, :, None] - 1) * cols) % (2 * nlon)
    phase = turn.astype(F32) * (math.pi / nlon)
    inside = (jnp.arange(wide) < lon).astype(F32)
    cphase, sphase = jnp.cos(phase) * inside, jnp.sin(phase) * inside
    con, son = cphase[:, :, :lon] * on[:, :, None], sphase[:, :, :lon] * on[:, :, None]
    keep = jnp.broadcast_to((step - on)[:, :, None], (steps, chunk, lon))
    wavenum = jnp.arange(KMAX)
    scale = jnp.where(wavenum == 0, 1.0 / nlon, 2.0 / nlon).astype(F32)
    weights = (wavenum < cut[:, :, None]).astype(F32) * scale * on[:, :, None]
    weights = jnp.concatenate([weights, weights], axis=2)

    u = np.zeros((padr, wide))
    u[:total, :lon] = source
    u = np.concatenate(split_np(u), axis=0)
    v = np.zeros((padr, lon))
    v[:total] = target
    vhi, vlo = split_np(v)
    v = jnp.asarray(np.concatenate([vhi, vhi, vlo], axis=0))
    angle = (np.arange(lon)[:, None] * np.arange(KMAX)[None, :] % nlon) * (2.0 * math.pi / nlon)
    table = np.concatenate([np.cos(angle), np.sin(angle)], axis=1)
    thi, tlo = split_np(table)
    ihi, ilo = np.ascontiguousarray(thi.T), np.ascontiguousarray(tlo.T)

    def whole(x):
        return pl.BlockSpec(x.shape, lambda i: (0,) * x.ndim)

    def stage(*shape):
        return pl.BlockSpec((1,) + shape, lambda i: (i,) + (0,) * len(shape))

    band = pl.BlockSpec((nf, chunk, nlev, lon), lambda i: (0, i, 0, 0))
    m = nf * chunk * nlev
    params = pltpu.CompilerParams(vmem_limit_bytes=60 * 1024 * 1024)
    u = jnp.asarray(u)
    tables = [u] + [jnp.asarray(x) for x in (thi, tlo, ihi, ilo)]
    n_off = len(ranks)
    vmem, far = pl.BlockSpec(memory_space=pltpu.VMEM), pl.BlockSpec(memory_space=pl.ANY)
    out = pl.pallas_call(
        functools.partial(first_kernel, ranks, 1.0 / (2.0 * dlon), 1.0 / (2.0 * dlat), chunk),
        in_specs=[far] + [vmem] * 5 + [far] * 5,
        out_specs=[far] * (n_off + 1),
        out_shape=[jax.ShapeDtypeStruct(fields.shape, F32)]
        + [jax.ShapeDtypeStruct((steps, 2 * r, m), F32) for r in ranks],
        scratch_shapes=[
            pltpu.VMEM(fields.shape, F32),
            pltpu.VMEM((nf, chunk + 2, nlev, wide), F32),
            pltpu.VMEM((2, nf, nlev, lon), F32),
            pltpu.VMEM((2, steps, nlev, 128), F32),
            pltpu.VMEM((2, steps, nlev, 128), F32),
        ]
        + [pltpu.VMEM((steps, 2 * r, m), F32) for r in ranks]
        + [
            pltpu.SemaphoreType.DMA,
            pltpu.SemaphoreType.DMA((2,)),
            pltpu.SemaphoreType.DMA((2,)),
            pltpu.SemaphoreType.DMA((2,)),
            pltpu.SemaphoreType.DMA((2,)),
            pltpu.SemaphoreType.DMA((n_off, steps)),
            pltpu.SemaphoreType.DMA((n_off, steps)),
        ]
        + [pltpu.VMEM(x.shape, BF16) for x in tables]
        + [pltpu.SemaphoreType.DMA((5,)), pltpu.VMEM(fields.shape, F32), pltpu.SemaphoreType.DMA((steps,))],
        compiler_params=pltpu.CompilerParams(
            vmem_limit_bytes=60 * 1024 * 1024, collective_id=0, has_side_effects=True
        ),
        name="tendency",
    )(fields, cosine, cphase, sphase, keep, weights, *tables)
    tend, got = out[0], out[1:]
    active = polar(lat_pos, lat_count, rows, chunk, jnp.arange(steps)).astype(jnp.int32)
    out = pl.pallas_call(
        functools.partial(second_kernel, ranks),
        grid=(steps,),
        in_specs=[pl.BlockSpec(memory_space=pltpu.SMEM), band, stage(chunk, lon), stage(chunk, lon), whole(v)]
        + [stage(2 * r, m) for r in ranks],
        out_specs=band,
        out_shape=jax.ShapeDtypeStruct(fields.shape, F32),
        compiler_params=params,
        name="projection",
    )(active, tend, con, son, v, *got)
    return jnp.transpose(out, (0, 2, 1, 3))


def solution(mesh):
    placed = (P(None, None, "lat", "lon"), P("lat"), P("lat"))
    return jax.shard_map(
        shards, mesh=mesh, in_specs=placed, out_specs=P(None, None, "lat", "lon"), check_vma=False
    )
```
